32 devices in a mesh: rcpt: 4 (over y, x), space: 8 (over z, core).
Axes of the slice: x: 2, y: 2, z: 4, core: 2. Of those that a mesh axis runs over, the one named last changes fastest.
Arguments:
- adjoint_end: float32 [32, 4, 256, 1024], P('rcpt', None, 'space'), may hold values from -6 to 6
- currents: bfloat16 [4, 2, 4, 256, 1024], P('rcpt', None, None, 'space'), may hold values from -0.29882812 to 0.29882812
- plan: int32 [4], replicated, may hold values from 0 to 3, as said below
- water_mask: int32 [256, 1024], P('space'), may hold values 0 or 1
- mixing: float32 [3, 256, 1024], P(None, 'space'), may hold values from 0.02 to 0.2
- decay: float32 [32], P('rcpt'), may hold values from 0.02 to 0.5
- obs_weight: float32 [4, 32], P(None, 'rcpt'), may hold values from 0.3 to 3
- release_cells: int32 [8, 32, 128], P('space'), may hold values from 0 to 32767
- profiles: float32 [8, 32, 512, 128], P(None, ('rcpt', 'space')), may hold values from -0.25 to 0.25
Outputs:
- adjoint_start: float32 [32, 4, 256, 1024], P('rcpt', None, 'space')
- sensitivity: float32 [8, 32, 32, 128], P(None, ('rcpt', 'space'))
The draws below stay inside these ranges and needn't reach their ends.
Inputs may be any that keep to these rules, and one draw needn't show every extreme that they name: 4 distinct store slots; hour h's currents are currents[plan[h]], held by rcpt index plan[h].
All inputs are finite; a program needn't handle non-finite values. No bound on the sum of `water_mask` on one device may be relied on, other than what follows from the above.
Results may differ from the reference program's by a relative error of at most 0.0003.
Values may be sent and summed in bfloat16 or wider, within the bound.
A program may use at most 256 MiB of HBM per device.

```python
import math
import jax
import jax.numpy as jnp
from jax import lax

CX = 32
NY = 1024
LEVELS = 4
HOURS = 4
CB = 128
P_SIZE = 128
RECEPTORS = 32
NS = 8
NX = 256
STORE = 4
BLK_STRIP = 32


def draw_plan(key, part):
    return jax.random.permutation(key, STORE)[:HOURS].astype(jnp.int32)


def touch_ends(array, own_key, least, largest):
    longest = array.shape.index(max(array.shape))
    spots = []
    for shift in (0, 1):
        where = [jax.random.randint(jax.random.fold_in(own_key, axis), (), 0, length) for axis, length in enumerate(array.shape)]
        where[longest] = (where[longest] + shift) % array.shape[longest]
        spots.append(tuple(where))
    return array.at[spots[0]].set(least).at[spots[1]].set(largest)


def block_levels(own_key, extent, pieces, least, largest):
    gain = 1.0
    for position, parts in pieces:
        steps = jax.random.uniform(jax.random.fold_in(jax.random.fold_in(own_key, 6), position), (parts,), jnp.float32, least / len(pieces), largest / len(pieces))
        gain = gain * jnp.repeat(jnp.exp(steps), extent[position] // parts).reshape((-1,) + (1,) * (len(extent) - 1 - position))
    return gain


def scatter_about(key, extent, width, reach, cuts=(), kind=jnp.bfloat16):
    array = width * jax.random.normal(key, extent, jnp.float32)
    if cuts:
        array = array * block_levels(key, extent, cuts, -0.22, 0.18)
    return jnp.clip(array, -reach, reach).astype(kind)


def setup_inputs(seed: int = 0) -> dict:
    key_list = jax.random.split(jax.random.key(seed), 10)
    adjoint_end = scatter_about(key_list[0], (RECEPTORS, LEVELS, NX, NY), 1.0, 6.0, ((0, 4), (2, 8)), jnp.float32)
    currents = jnp.clip(jax.random.uniform(key_list[1], (STORE, 2, LEVELS, NX, NY), jnp.float32, -0.29882812, 0.29882812) * block_levels(key_list[1], (STORE, 2, LEVELS, NX, NY), ((0, 4), (3, 8)), -0.4, 0.0), -0.29882812, 0.29882812).astype(jnp.bfloat16)
    plan = draw_plan(jax.random.fold_in(key_list[9], 71), 0)
    water_mask = touch_ends((jax.random.randint(key_list[3], (NX, NY), 0, 8) < 7).astype(jnp.int32), jax.random.fold_in(key_list[3], 1), 0, 1)
    mixing = jnp.clip(0.02 + 0.18 * jax.random.uniform(key_list[4], (LEVELS - 1, NX, NY), jnp.float32) ** block_levels(key_list[4], (LEVELS - 1, NX, NY), ((1, 8),), -0.2, 0.2), 0.02, 0.2)
    decay = jnp.clip(jnp.exp(math.log(0.5) - 3.218876 * jax.random.uniform(key_list[5], (RECEPTORS,), jnp.float32) ** block_levels(key_list[5], (RECEPTORS,), ((0, 4),), -0.2, 0.2)), 0.02, 0.5)
    obs_weight = jnp.clip(jnp.exp(math.log(3.0) - 2.3025851 * jax.random.uniform(key_list[6], (HOURS, RECEPTORS), jnp.float32) ** block_levels(key_list[6], (HOURS, RECEPTORS), ((1, 4),), -0.2, 0.2)), 0.3, 3.0)
    release_cells = touch_ends(jax.random.randint(key_list[7], (NS, BLK_STRIP, CB), 0, CX * NY), jax.random.fold_in(key_list[7], 1), 0, (CX * NY) - 1).astype(jnp.int32)
    profiles = scatter_about(key_list[8], (NS, BLK_STRIP, LEVELS * CB, P_SIZE), (LEVELS * CB) ** -0.5, 0.25, ((1, 32),), jnp.float32)
    return dict(adjoint_end=adjoint_end, currents=currents, plan=plan, water_mask=water_mask, mixing=mixing, decay=decay, obs_weight=obs_weight, release_cells=release_cells, profiles=profiles)


diffusion_number = 0.08


def transport(padded, water, current, mixing):
    center = padded[:, :, 1:-1, 1:-1]
    along = current[0].astype(jnp.float32)
    across = current[1].astype(jnp.float32)
    inner = water[1:-1, 1:-1]
    weight_down = (jax.nn.relu(along) + diffusion_number) * water[2:, 1:-1]
    weight_up = (jax.nn.relu(-along) + diffusion_number) * water[:-2, 1:-1]
    weight_right = (jax.nn.relu(across) + diffusion_number) * water[1:-1, 2:]
    weight_left = (jax.nn.relu(-across) + diffusion_number) * water[1:-1, :-2]
    moved = center + weight_down * (padded[:, :, 2:, 1:-1] - center)
    moved = moved + weight_up * (padded[:, :, :-2, 1:-1] - center)
    moved = moved + weight_right * (padded[:, :, 1:-1, 2:] - center)
    moved = moved + weight_left * (padded[:, :, 1:-1, :-2] - center)
    moved = moved * inner
    vertical_flux = mixing * (moved[:, 1:] - moved[:, :-1])
    zeros = jnp.zeros_like(moved[:, :1])
    return moved + jnp.concatenate([vertical_flux, zeros], 1) - jnp.concatenate([zeros, vertical_flux], 1)


def reference(adjoint_end, currents, plan, water_mask, mixing, decay, obs_weight, release_cells, profiles):
    water = jnp.pad(water_mask.astype(jnp.float32), 1)
    inner = water[1:-1, 1:-1]
    source = inner * adjoint_end
    keep = (1.0 - decay)[:, None, None, None]
    field = adjoint_end
    for hour_index in reversed(range(HOURS)):
        current = lax.dynamic_index_in_dim(currents, plan[hour_index], 0, keepdims=False)
        padded = jnp.pad(field, ((0, 0), (0, 0), (1, 1), (1, 1)))
        mixed = transport(padded, water, current, mixing)
        field = keep * mixed + obs_weight[hour_index][:, None, None, None] * source
    strips = field.reshape(RECEPTORS, LEVELS, NS, CX * NY)
    strip_ids = jnp.arange(NS, dtype=jnp.int32)[:, None, None]
    samples = strips[:, :, strip_ids, release_cells]
    samples = jnp.transpose(samples, (0, 2, 3, 1, 4)).reshape(RECEPTORS, NS, BLK_STRIP, LEVELS * CB)
    sensitivity = jnp.einsum("rsbk,sbkp->sbrp", samples, profiles, precision=lax.Precision.HIGHEST)
    return field, sensitivity
```

```python
import functools

import jax
import jax.numpy as jnp
from jax import lax
from jax.experimental import pallas as pl
from jax.experimental.pallas import tpu as pltpu
from jax.sharding import PartitionSpec as P

HOURS = 4
LANES = 128
SUBROWS = 16
MESH = pl.DeviceIdType.MESH
VMEM_LIMIT = 48 * 1024 * 1024

diffusion_number = 0.08


def steps_kernel(
    batches, strips,
    plan_ref, decay_ref, obs_ref, water_ref, mix_ref, adj_hbm, cur_hbm,
    out_hbm,
    cur_buf, raw, fa, fb, src, halo, water_halo, gate, weight,
    cur_send, cur_recv, cur_own, halo_send, halo_recv, wat_send, wat_recv, in_sem, out_sem,
):
    recv, levels, rows, width = adj_hbm.shape
    slots = cur_hbm.shape[0]
    me = lax.axis_index("rcpt")
    strip = lax.axis_index("space")
    has_up = strip > 0
    has_down = strip < strips - 1

    barrier = pltpu.get_barrier_semaphore()
    for d in range(1, batches):
        pl.semaphore_signal(
            barrier, inc=1, device_id={"rcpt": lax.rem(me + d, batches)}, device_id_type=MESH
        )

    @pl.when(has_up)
    def _():
        pl.semaphore_signal(barrier, inc=1, device_id={"space": strip - 1}, device_id_type=MESH)

    @pl.when(has_down)
    def _():
        pl.semaphore_signal(barrier, inc=1, device_id={"space": strip + 1}, device_id_type=MESH)

    loads = [
        pltpu.make_async_copy(adj_hbm.at[r], raw.at[r], in_sem.at[r]) for r in range(recv)
    ]
    for load in loads:
        load.start()
    own_slots = cur_buf.at[pl.ds(me * slots, slots)]
    own_copy = pltpu.make_async_copy(cur_hbm, own_slots, cur_own)
    own_copy.start()

    peers = batches - 1 + has_up.astype(jnp.int32) + has_down.astype(jnp.int32)
    pl.semaphore_wait(barrier, peers)

    spread = []
    for d in range(1, batches):
        copy = pltpu.make_async_remote_copy(
            src_ref=cur_hbm, dst_ref=own_slots,
            send_sem=cur_send.at[d - 1], recv_sem=cur_recv.at[d - 1],
            device_id={"rcpt": lax.rem(me + d, batches)}, device_id_type=MESH,
        )
        copy.start()
        spread.append(copy)

    def water_copies():
        up = pltpu.make_async_remote_copy(
            src_ref=water_ref.at[pl.ds(0, 8)], dst_ref=water_halo.at[1],
            send_sem=wat_send.at[0], recv_sem=wat_recv.at[0],
            device_id={"space": strip - 1}, device_id_type=MESH,
        )
        down = pltpu.make_async_remote_copy(
            src_ref=water_ref.at[pl.ds(rows - 8, 8)], dst_ref=water_halo.at[0],
            send_sem=wat_send.at[1], recv_sem=wat_recv.at[1],
            device_id={"space": strip + 1}, device_id_type=MESH,
        )
        return up, down

    def halo_copies(step, field):
        up = pltpu.make_async_remote_copy(
            src_ref=field.at[:, 0], dst_ref=halo.at[step, 1],
            send_sem=halo_send.at[step, 0], recv_sem=halo_recv.at[step, 0],
            device_id={"space": strip - 1}, device_id_type=MESH,
        )
        down = pltpu.make_async_remote_copy(
            src_ref=field.at[:, rows - 1], dst_ref=halo.at[step, 0],
            send_sem=halo_send.at[step, 1], recv_sem=halo_recv.at[step, 1],
            device_id={"space": strip + 1}, device_id_type=MESH,
        )
        return up, down

    def start(copies):
        up, down = copies

        @pl.when(has_up)
        def _():
            up.start()

        @pl.when(has_down)
        def _():
            down.start()

    def finish(copies):
        up, down = copies

        @pl.when(has_up)
        def _():
            up.wait_send()
            down.wait_recv()

        @pl.when(has_down)
        def _():
            down.wait_send()
            up.wait_recv()

    water_pair = water_copies()
    start(water_pair)

    for load in loads:
        load.wait()

    def arrange(t, _):
        for level in range(levels):
            block = raw[:, level, pl.ds(pl.multiple_of(t * 8, 8), 8), :]
            fa[level, pl.ds(t * 8, 8)] = jnp.swapaxes(block, 0, 1)
        return 0

    lax.fori_loop(0, rows // 8, arrange, 0)
    pair = halo_copies(0, fa)
    start(pair)

    @pl.when(jnp.logical_not(has_up))
    def _():
        water_halo[0] = jnp.zeros_like(water_halo[0])
        for step in range(HOURS):
            halo[step, 0] = jnp.zeros_like(halo[step, 0])

    @pl.when(jnp.logical_not(has_down))
    def _():
        water_halo[1] = jnp.zeros_like(water_halo[1])
        for step in range(HOURS):
            halo[step, 1] = jnp.zeros_like(halo[step, 1])

    finish(water_pair)
    inner = water_ref[...].astype(jnp.float32)
    above = water_halo[0, 7:8, :].astype(jnp.float32)
    below = water_halo[1, 0:1, :].astype(jnp.float32)
    row_at = lax.broadcasted_iota(jnp.int32, (rows, width), 0)
    col_at = lax.broadcasted_iota(jnp.int32, (rows, width), 1)
    up_water = jnp.where(row_at == 0, above, pltpu.roll(inner, 1, 0))
    down_water = jnp.where(row_at == rows - 1, below, pltpu.roll(inner, rows - 1, 0))
    left_water = jnp.where(col_at == 0, 0.0, pltpu.roll(inner, 1, 1))
    right_water = jnp.where(col_at == width - 1, 0.0, pltpu.roll(inner, width - 1, 1))
    gate[0] = inner
    gate[1] = inner * up_water
    gate[2] = inner * down_water
    gate[3] = inner * left_water
    gate[4] = inner * right_water

    def make_source(i, _):
        here = gate[0, pl.ds(i, 1), :]
        for level in range(levels):
            src[level, i] = fa[level, i] * here
        return 0

    lax.fori_loop(0, rows, make_source, 0)

    sub = lax.broadcasted_iota(jnp.int32, (recv, LANES), 0)

    def per_receptor(read):
        value = jnp.zeros((recv, LANES), jnp.float32)
        for r in range(recv):
            value = jnp.where(sub == r, read(r), value)
        return jnp.concatenate([value] * (width // LANES), 1)

    keep = per_receptor(lambda r: 1.0 - decay_ref[r])

    own_copy.wait()
    for copy in spread:
        copy.wait()

    def make_weights(hour):
        slot = plan_ref[hour]

        def tile(t, _):
            at = pl.ds(pl.multiple_of(t * SUBROWS, SUBROWS), SUBROWS)
            for level in range(levels):
                along = cur_buf[slot, 0, level, at, :].astype(jnp.float32)
                across = cur_buf[slot, 1, level, at, :].astype(jnp.float32)
                up = (jnp.maximum(-along, 0.0) + diffusion_number) * gate[1, at, :]
                down = (jnp.maximum(along, 0.0) + diffusion_number) * gate[2, at, :]
                left = (jnp.maximum(-across, 0.0) + diffusion_number) * gate[3, at, :]
                right = (jnp.maximum(across, 0.0) + diffusion_number) * gate[4, at, :]
                weight[0, level, at, :] = gate[0, at, :] - ((up + down) + (left + right))
                weight[1, level, at, :] = up
                weight[2, level, at, :] = down
                weight[3, level, at, :] = left
                weight[4, level, at, :] = right
            return 0

        lax.fori_loop(0, rows // SUBROWS, tile, 0)

    def do_row(fin, fout, i, upper, lower, obs):
        at = pl.ds(i, 1)

        def moved_at(level):
            center = fin[level, i]
            out = center * weight[0, level, at, :]
            out = out + upper(level) * weight[1, level, at, :]
            out = out + lower(level) * weight[2, level, at, :]
            out = out + pltpu.roll(center, 1, 1) * weight[3, level, at, :]
            return out + pltpu.roll(center, width - 1, 1) * weight[4, level, at, :]

        moved = moved_at(0)
        flux = None
        for level in range(levels):
            mixed = moved
            if flux is not None:
                mixed = mixed - flux
            if level < levels - 1:
                following = moved_at(level + 1)
                flux = mix_ref[level, at, :] * (following - moved)
                mixed = mixed + flux
                moved = following
            fout[level, i] = keep * mixed + obs * src[level, i]

    for step in range(HOURS):
        hour = HOURS - 1 - step
        fin, fout = (fa, fb) if step % 2 == 0 else (fb, fa)
        make_weights(hour)
        obs = per_receptor(lambda r: obs_ref[hour, r])
        finish(pair)
        do_row(
            fin, fout, 0,
            lambda level: halo[step, 0, level], lambda level: fin[level, 1], obs,
        )
        do_row(
            fin, fout, rows - 1,
            lambda level: fin[level, rows - 2], lambda level: halo[step, 1, level], obs,
        )
        if step < HOURS - 1:
            pair = halo_copies(step + 1, fout)
            start(pair)

        def interior(i, _):
            do_row(
                fin, fout, i,
                lambda level: fin[level, i - 1], lambda level: fin[level, i + 1], obs,
            )
            return 0

        lax.fori_loop(1, rows - 1, interior, 0)

    done = pltpu.make_async_copy(fout, out_hbm, out_sem)
    done.start()
    done.wait()


def run_steps(batches, strips, plan, decay, obs_weight, water, mixing, adjoint_end, currents):
    recv, levels, rows, width = adjoint_end.shape
    field = (levels, rows, recv, width)
    slots = currents.shape[0]
    vmem = pl.BlockSpec(memory_space=pltpu.VMEM)
    smem = pl.BlockSpec(memory_space=pltpu.SMEM)
    hbm = pl.BlockSpec(memory_space=pl.ANY)
    dma = pltpu.SemaphoreType.DMA
    return pl.pallas_call(
        functools.partial(steps_kernel, batches, strips),
        out_shape=jax.ShapeDtypeStruct(field, jnp.float32),
        in_specs=[smem, smem, smem, vmem, vmem, hbm, hbm],
        out_specs=hbm,
        scratch_shapes=[
            pltpu.VMEM((batches * slots,) + currents.shape[1:], currents.dtype),
            pltpu.VMEM(adjoint_end.shape, jnp.float32),
            pltpu.VMEM(field, jnp.float32),
            pltpu.VMEM(field, jnp.float32),
            pltpu.VMEM(field, jnp.float32),
            pltpu.VMEM((HOURS, 2, levels, recv, width), jnp.float32),
            pltpu.VMEM((2, 8, width), jnp.int32),
            pltpu.VMEM((5, rows, width), jnp.float32),
            pltpu.VMEM((5, levels, rows, width), jnp.float32),
            dma((batches - 1,)),
            dma((batches - 1,)),
            dma,
            dma((HOURS, 2)),
            dma((HOURS, 2)),
            dma((2,)),
            dma((2,)),
            dma((recv,)),
            dma,
        ],
        compiler_params=pltpu.CompilerParams(
            collective_id=0, has_side_effects=True, vmem_limit_bytes=VMEM_LIMIT
        ),
        name="transport_steps",
    )(plan, decay, obs_weight, water, mixing, adjoint_end, currents)


def sample_kernel(cells_ref, field_hbm, out_hbm, samples_ref, field, native, in_sem, out_sem):
    levels, rows, recv, width = field.shape
    blocks, block_cells = cells_ref.shape
    tiles = width // LANES
    load = pltpu.make_async_copy(field_hbm, field, in_sem)
    load.start()
    load.wait()

    def arrange(t, _):
        for level in range(levels):
            block = field[level, pl.ds(t * 8, 8)]
            native[:, level, pl.ds(pl.multiple_of(t * 8, 8), 8), :] = jnp.swapaxes(block, 0, 1)
        return 0

    lax.fori_loop(0, rows // 8, arrange, 0)
    stores = [
        pltpu.make_async_copy(native.at[r], out_hbm.at[r], out_sem.at[r]) for r in range(recv)
    ]
    for store in stores:
        store.start()

    group = 2 if blocks % 2 == 0 else 1

    def gather(g, _):
        lane, tile = [], []
        for k in range(group):
            cell = jnp.broadcast_to(cells_ref[pl.ds(g * group + k, 1), :], (recv, block_cells))
            lane.append(lax.rem(cell, LANES))
            tile.append(lax.div(cell, LANES))

        def row(i, totals):
            totals = list(totals)
            for c in range(tiles):
                hit = [tile[k] == i * tiles + c for k in range(group)]
                for level in range(levels):
                    values = field[level, i, :, c * LANES : (c + 1) * LANES]
                    for k in range(group):
                        picked = jnp.take_along_axis(
                            values, lane[k], axis=1, mode="promise_in_bounds"
                        )
                        at = k * levels + level
                        totals[at] = jnp.where(hit[k], picked, totals[at])
            return tuple(totals)

        zero = jnp.zeros((recv, block_cells), jnp.float32)
        totals = lax.fori_loop(0, rows, row, (zero,) * (group * levels))
        for k in range(group):
            for level in range(levels):
                samples_ref[
                    g * group + k, :, level * block_cells : (level + 1) * block_cells
                ] = totals[k * levels + level]
        return 0

    lax.fori_loop(0, blocks // group, gather, 0)
    for store in stores:
        store.wait()


def run_samples(cells, field):
    levels, rows, recv, width = field.shape
    blocks, block_cells = cells.shape
    vmem = pl.BlockSpec(memory_space=pltpu.VMEM)
    hbm = pl.BlockSpec(memory_space=pl.ANY)
    return pl.pallas_call(
        sample_kernel,
        out_shape=(
            jax.ShapeDtypeStruct((recv, levels, rows, width), jnp.float32),
            jax.ShapeDtypeStruct((blocks, recv, levels * block_cells), jnp.float32),
        ),
        in_specs=[vmem, hbm],
        out_specs=(hbm, vmem),
        scratch_shapes=[
            pltpu.VMEM(field.shape, jnp.float32),
            pltpu.VMEM((recv, levels, rows, width), jnp.float32),
            pltpu.SemaphoreType.DMA,
            pltpu.SemaphoreType.DMA((recv,)),
        ],
        compiler_params=pltpu.CompilerParams(vmem_limit_bytes=VMEM_LIMIT),
        name="release_samples",
    )(cells, field)


def contract_kernel(samples_ref, profiles_ref, out_ref):
    batches, own, recv, depth = samples_ref.shape
    for b in range(own):
        left = samples_ref[:, b].reshape(batches * recv, depth)
        out_ref[b] = jnp.dot(
            left, profiles_ref[b], precision=lax.Precision.HIGHEST,
            preferred_element_type=jnp.float32,
        )


def run_contract(gathered, profiles):
    batches, strips, own, recv, depth = gathered.shape
    scenarios = profiles.shape[-1]
    return pl.pallas_call(
        contract_kernel,
        grid=(strips,),
        out_shape=jax.ShapeDtypeStruct((strips, own, batches * recv, scenarios), jnp.float32),
        in_specs=[
            pl.BlockSpec((batches, None, own, recv, depth), lambda s: (0, s, 0, 0, 0)),
            pl.BlockSpec((None, own, depth, scenarios), lambda s: (s, 0, 0, 0)),
        ],
        out_specs=pl.BlockSpec((None, own, batches * recv, scenarios), lambda s: (s, 0, 0, 0)),
        compiler_params=pltpu.CompilerParams(vmem_limit_bytes=VMEM_LIMIT),
        name="scenario_response",
    )(gathered, profiles)


def on_device(
    adjoint_end, currents, plan, water_mask, mixing, decay, obs_weight, release_cells, profiles
):
    batches = lax.axis_size("rcpt")
    strips = lax.axis_size("space")
    stepped = run_steps(
        batches, strips, plan, decay, obs_weight, water_mask, mixing, adjoint_end, currents
    )
    field, samples = run_samples(release_cells[0], stepped)
    gathered = lax.all_to_all(samples, ("rcpt", "space"), split_axis=0, concat_axis=0, tiled=True)
    own = samples.shape[0] // (batches * strips)
    gathered = gathered.reshape((batches, strips, own) + samples.shape[1:])
    return (field, run_contract(gathered, profiles))


def solution(mesh):
    placed = (
        P("rcpt", None, "space", None),
        P("rcpt", None, None, "space", None),
        P(),
        P("space", None),
        P(None, "space", None),
        P("rcpt"),
        P(None, "rcpt"),
        P("space", None, None),
        P(None, ("rcpt", "space"), None, None),
    )
    return jax.shard_map(
        on_device,
        mesh=mesh,
        in_specs=placed,
        out_specs=(P("rcpt", None, "space", None), P(None, ("rcpt", "space"), None, None)),
        check_vma=False,
    )
```

```python
import functools

import jax
import jax.numpy as jnp
from jax import lax
from jax.experimental import pallas as pl
from jax.experimental.pallas import tpu as pltpu
from jax.sharding import PartitionSpec as P

HOURS = 4
LANES = 128
SUBROWS = 16
MESH = pl.DeviceIdType.MESH
VMEM_LIMIT = 48 * 1024 * 1024

diffusion_number = 0.08


def steps_kernel(
    batches, strips,
    plan_hbm, decay_hbm, obs_hbm, water_hbm, mix_hbm, adj_hbm, cur_hbm,
    out_hbm,
    plan_ref, decay_ref, obs_ref, water_ref, mix_ref,
    cur_parts, raw, fa, fb, src, halo, water_halo, gate, weight,
    cur_send, cur_recv, cur_own, halo_send, halo_recv, wat_send, wat_recv, in_sem, arg_sem, out_sem,
):
    recv, levels, rows, width = adj_hbm.shape
    slots = cur_hbm.shape[0]
    me = lax.axis_index("rcpt")
    strip = lax.axis_index("space")
    has_up = strip > 0
    has_down = strip < strips - 1

    barrier = pltpu.get_barrier_semaphore()
    for d in range(1, batches):
        pl.semaphore_signal(
            barrier, inc=1, device_id={"rcpt": lax.rem(me + d, batches)}, device_id_type=MESH
        )

    @pl.when(has_up)
    def _():
        pl.semaphore_signal(barrier, inc=1, device_id={"space": strip - 1}, device_id_type=MESH)

    @pl.when(has_down)
    def _():
        pl.semaphore_signal(barrier, inc=1, device_id={"space": strip + 1}, device_id_type=MESH)

    loads = [
        pltpu.make_async_copy(adj_hbm.at[r], raw.at[r], in_sem.at[r]) for r in range(recv)
    ]
    for load in loads:
        load.start()
    pairs = (
        (water_hbm, water_ref), (mix_hbm, mix_ref), (plan_hbm, plan_ref),
        (decay_hbm, decay_ref), (obs_hbm, obs_ref),
    )
    args = [
        pltpu.make_async_copy(there, here, arg_sem.at[k]) for k, (there, here) in enumerate(pairs)
    ]
    for arg in args:
        arg.start()
    parts = len(cur_parts)
    part_rows = rows // parts

    def slots_of(owner, part, component=None):
        at = pl.ds(owner * slots, slots)
        return cur_parts[part].at[at] if component is None else cur_parts[part].at[at, component]

    def stored(part):
        return cur_hbm.at[:, :, :, pl.ds(part * part_rows, part_rows)]

    own_copies = [
        pltpu.make_async_copy(stored(part), slots_of(me, part), cur_own.at[part])
        for part in range(parts)
    ]
    for copy in own_copies:
        copy.start()

    peers = batches - 1 + has_up.astype(jnp.int32) + has_down.astype(jnp.int32)
    pl.semaphore_wait(barrier, peers)

    def send(part, k, source, target, peer):
        return pltpu.make_async_remote_copy(
            src_ref=source, dst_ref=target,
            send_sem=cur_send.at[part, k], recv_sem=cur_recv.at[part, k],
            device_id={"rcpt": peer}, device_id_type=MESH,
        )

    square = batches == 4
    if square:
        side = me + 1 - 2 * lax.rem(me, 2)
        other = lax.rem(me + 2, batches)
        partners = (side, other)
    else:
        partners = tuple(lax.rem(me + d, batches) for d in range(1, batches))
    spread = [
        [
            send(
                part, k, stored(part), slots_of(me, part), peer,
            )
            for k, peer in enumerate(partners)
        ]
        for part in range(parts)
    ]
    passed = []
    if square:
        passed = [
            [
                send(part, 2, slots_of(other, part, 0), slots_of(other, part, 0), side),
                send(part, 3, slots_of(side, part, 1), slots_of(side, part, 1), other),
            ]
            for part in range(parts)
        ]
    for copies in spread:
        for copy in copies:
            copy.start()

    def pass_on(part):
        if square:
            spread[part][1].wait_recv()
            passed[part][0].start()
            spread[part][0].wait_recv()
            passed[part][1].start()

    def arrived(part):
        if square:
            for copy in passed[part]:
                copy.wait_recv()
        else:
            for copy in spread[part]:
                copy.wait_recv()

    def water_copies():
        up = pltpu.make_async_remote_copy(
            src_ref=water_hbm.at[pl.ds(0, 8)], dst_ref=water_halo.at[1],
            send_sem=wat_send.at[0], recv_sem=wat_recv.at[0],
            device_id={"space": strip - 1}, device_id_type=MESH,
        )
        down = pltpu.make_async_remote_copy(
            src_ref=water_hbm.at[pl.ds(rows - 8, 8)], dst_ref=water_halo.at[0],
            send_sem=wat_send.at[1], recv_sem=wat_recv.at[1],
            device_id={"space": strip + 1}, device_id_type=MESH,
        )
        return up, down

    def halo_copies(step, field):
        up = pltpu.make_async_remote_copy(
            src_ref=field.at[:, 0], dst_ref=halo.at[step, 1],
            send_sem=halo_send.at[step, 0], recv_sem=halo_recv.at[step, 0],
            device_id={"space": strip - 1}, device_id_type=MESH,
        )
        down = pltpu.make_async_remote_copy(
            src_ref=field.at[:, rows - 1], dst_ref=halo.at[step, 0],
            send_sem=halo_send.at[step, 1], recv_sem=halo_recv.at[step, 1],
            device_id={"space": strip + 1}, device_id_type=MESH,
        )
        return up, down

    def start(copies):
        up, down = copies

        @pl.when(has_up)
        def _():
            up.start()

        @pl.when(has_down)
        def _():
            down.start()

    def finish(copies):
        up, down = copies

        @pl.when(has_up)
        def _():
            up.wait_send()
            down.wait_recv()

        @pl.when(has_down)
        def _():
            down.wait_send()
            up.wait_recv()

    water_pair = water_copies()
    start(water_pair)

    for load in loads:
        load.wait()

    def arrange(t, _):
        for level in range(levels):
            block = raw[:, level, pl.ds(pl.multiple_of(t * 8, 8), 8), :]
            fa[level, pl.ds(t * 8, 8)] = jnp.swapaxes(block, 0, 1)
        return 0

    lax.fori_loop(0, rows // 8, arrange, 0)
    pair = halo_copies(0, fa)
    start(pair)

    @pl.when(jnp.logical_not(has_up))
    def _():
        water_halo[0] = jnp.zeros_like(water_halo[0])
        for step in range(HOURS):
            halo[step, 0] = jnp.zeros_like(halo[step, 0])

    @pl.when(jnp.logical_not(has_down))
    def _():
        water_halo[1] = jnp.zeros_like(water_halo[1])
        for step in range(HOURS):
            halo[step, 1] = jnp.zeros_like(halo[step, 1])

    for arg in args:
        arg.wait()
    finish(water_pair)
    inner = water_ref[...].astype(jnp.float32)
    above = water_halo[0, 7:8, :].astype(jnp.float32)
    below = water_halo[1, 0:1, :].astype(jnp.float32)
    row_at = lax.broadcasted_iota(jnp.int32, (rows, width), 0)
    col_at = lax.broadcasted_iota(jnp.int32, (rows, width), 1)
    up_water = jnp.where(row_at == 0, above, pltpu.roll(inner, 1, 0))
    down_water = jnp.where(row_at == rows - 1, below, pltpu.roll(inner, rows - 1, 0))
    left_water = jnp.where(col_at == 0, 0.0, pltpu.roll(inner, 1, 1))
    right_water = jnp.where(col_at == width - 1, 0.0, pltpu.roll(inner, width - 1, 1))
    gate[0] = inner
    gate[1] = inner * up_water
    gate[2] = inner * down_water
    gate[3] = inner * left_water
    gate[4] = inner * right_water

    def make_source(i, _):
        here = gate[0, pl.ds(i, 1), :]
        for level in range(levels):
            src[level, i] = fa[level, i] * here
        return 0

    lax.fori_loop(0, rows, make_source, 0)

    sub = lax.broadcasted_iota(jnp.int32, (recv, LANES), 0)

    def per_receptor(read):
        value = jnp.zeros((recv, LANES), jnp.float32)
        for r in range(recv):
            value = jnp.where(sub == r, read(r), value)
        return jnp.concatenate([value] * (width // LANES), 1)

    keep = per_receptor(lambda r: 1.0 - decay_ref[r])

    def make_weights(part):
        buffer = cur_parts[part]

        def tile(t, _):
            held = pl.ds(pl.multiple_of(t * SUBROWS, SUBROWS), SUBROWS)
            at = pl.ds(pl.multiple_of(part * part_rows + t * SUBROWS, SUBROWS), SUBROWS)
            for hour in range(HOURS):
                slot = plan_ref[hour]
                for level in range(levels):
                    along = buffer[slot, 0, level, held, :].astype(jnp.float32)
                    across = buffer[slot, 1, level, held, :].astype(jnp.float32)
                    up = (jnp.maximum(-along, 0.0) + diffusion_number) * gate[1, at, :]
                    down = (jnp.maximum(along, 0.0) + diffusion_number) * gate[2, at, :]
                    left = (jnp.maximum(-across, 0.0) + diffusion_number) * gate[3, at, :]
                    right = (jnp.maximum(across, 0.0) + diffusion_number) * gate[4, at, :]
                    middle = gate[0, at, :] - ((up + down) + (left + right))
                    for k, value in enumerate((middle, up, down, left, right)):
                        weight[hour, k, level, at, :] = value
            return 0

        lax.fori_loop(0, part_rows // SUBROWS, tile, 0)

    def do_row(hour, fin, fout, i, upper, lower, obs):
        at = pl.ds(i, 1)

        def moved_at(level):
            center = fin[level, i]
            out = center * weight[hour, 0, level, at, :]
            out = out + upper(level) * weight[hour, 1, level, at, :]
            out = out + lower(level) * weight[hour, 2, level, at, :]
            out = out + pltpu.roll(center, 1, 1) * weight[hour, 3, level, at, :]
            return out + pltpu.roll(center, width - 1, 1) * weight[hour, 4, level, at, :]

        moved = moved_at(0)
        flux = None
        for level in range(levels):
            mixed = moved
            if flux is not None:
                mixed = mixed - flux
            if level < levels - 1:
                following = moved_at(level + 1)
                flux = mix_ref[level, at, :] * (following - moved)
                mixed = mixed + flux
                moved = following
            fout[level, i] = keep * mixed + obs * src[level, i]

    seen = [per_receptor(lambda r, h=h: obs_ref[h, r]) for h in range(HOURS)]

    def buffers(step):
        return (fa, fb) if step % 2 == 0 else (fb, fa)

    def span(step, low, high):
        hour = HOURS - 1 - step
        fin, fout = buffers(step)

        def body(i, _):
            do_row(
                hour, fin, fout, i,
                lambda level: fin[level, i - 1], lambda level: fin[level, i + 1], seen[hour],
            )
            return 0

        if low < high:
            lax.fori_loop(low, high, body, 0)

    def first_row(step):
        hour = HOURS - 1 - step
        fin, fout = buffers(step)
        do_row(
            hour, fin, fout, 0,
            lambda level: halo[step, 0, level], lambda level: fin[level, 1], seen[hour],
        )

    def last_row(step):
        hour = HOURS - 1 - step
        fin, fout = buffers(step)
        do_row(
            hour, fin, fout, rows - 1,
            lambda level: fin[level, rows - 2], lambda level: halo[step, 1, level], seen[hour],
        )

    for copy in own_copies:
        copy.wait()
    pass_on(0)
    for part in range(parts):
        arrived(part)
        if part < parts - 1:
            make_weights(part)
            for step in range(HOURS):
                span(step, step + 1, part_rows - 1 - step)
                if step == 0:
                    pass_on(part + 1)
    make_weights(parts - 1)
    early = parts > 1
    for step in range(HOURS):
        finish(pair)
        first_row(step)
        last_row(step)
        if step < HOURS - 1:
            pair = halo_copies(step + 1, buffers(step)[1])
            start(pair)
        if early:
            span(step, 1, step + 1)
            span(step, max(part_rows - 1 - step, step + 1), rows - 1)
        else:
            span(step, 1, rows - 1)
    for copies in spread + passed:
        for copy in copies:
            copy.wait_send()

    fout = buffers(HOURS - 1)[1]
    done = pltpu.make_async_copy(fout, out_hbm, out_sem)
    done.start()
    done.wait()


def run_steps(batches, strips, plan, decay, obs_weight, water, mixing, adjoint_end, currents):
    recv, levels, rows, width = adjoint_end.shape
    field = (levels, rows, recv, width)
    slots = currents.shape[0]
    parts = 2 if rows % (2 * SUBROWS) == 0 else 1
    hbm = pl.BlockSpec(memory_space=pl.ANY)
    dma = pltpu.SemaphoreType.DMA
    return pl.pallas_call(
        functools.partial(steps_kernel, batches, strips),
        out_shape=jax.ShapeDtypeStruct(field, jnp.float32),
        in_specs=[hbm] * 7,
        out_specs=hbm,
        scratch_shapes=[
            pltpu.SMEM(plan.shape, jnp.int32),
            pltpu.SMEM(decay.shape, jnp.float32),
            pltpu.SMEM(obs_weight.shape, jnp.float32),
            pltpu.VMEM(water.shape, jnp.int32),
            pltpu.VMEM(mixing.shape, jnp.float32),
            [
                pltpu.VMEM(
                    (batches * slots, 2, levels, rows // parts, width), currents.dtype
                )
            ]
            * parts,
            pltpu.VMEM(adjoint_end.shape, jnp.float32),
            pltpu.VMEM(field, jnp.float32),
            pltpu.VMEM(field, jnp.float32),
            pltpu.VMEM(field, jnp.float32),
            pltpu.VMEM((HOURS, 2, levels, recv, width), jnp.float32),
            pltpu.VMEM((2, 8, width), jnp.int32),
            pltpu.VMEM((5, rows, width), jnp.float32),
            pltpu.VMEM((HOURS, 5, levels, rows, width), jnp.float32),
            dma((parts, max(batches - 1, 4))),
            dma((parts, max(batches - 1, 4))),
            dma((parts,)),
            dma((HOURS, 2)),
            dma((HOURS, 2)),
            dma((2,)),
            dma((2,)),
            dma((recv,)),
            dma((5,)),
            dma,
        ],
        compiler_params=pltpu.CompilerParams(
            collective_id=0, has_side_effects=True, vmem_limit_bytes=VMEM_LIMIT
        ),
        name="transport_steps",
    )(plan, decay, obs_weight, water, mixing, adjoint_end, currents)


def sample_kernel(
    cells_hbm, field_hbm, out_hbm, samples_ref,
    cells_ref, field, native, by_cell, picked, places, places_ref,
    cell_sem, place_sem, in_sem, out_sem,
):
    levels, rows, recv, width = field.shape
    blocks, block_cells = cells_ref.shape
    tiles = width // LANES
    packed = LANES // (levels * recv)
    load = pltpu.make_async_copy(field_hbm, field, in_sem)
    load.start()
    cell_load = pltpu.make_async_copy(cells_hbm, cells_ref, cell_sem)
    cell_load.start()
    cell_load.wait()
    cells = cells_ref[...]
    tile = lax.div(cells, LANES)
    places[...] = lax.div(tile, packed) * LANES + lax.rem(cells, LANES)
    place_copy = pltpu.make_async_copy(places, places_ref, place_sem)
    place_copy.start()
    load.wait()

    def arrange(t, _):
        for level in range(levels):
            block = field[level, pl.ds(t * 8, 8)]
            native[:, level, pl.ds(pl.multiple_of(t * 8, 8), 8), :] = jnp.swapaxes(block, 0, 1)
        return 0

    lax.fori_loop(0, rows // 8, arrange, 0)
    stores = [
        pltpu.make_async_copy(native.at[r], out_hbm.at[r], out_sem.at[r]) for r in range(recv)
    ]
    for store in stores:
        store.start()

    groups = tiles // packed

    def turn(i, _):
        for g in range(groups):
            stack = jnp.concatenate(
                [
                    field[level, i, :, (g * packed + q) * LANES : (g * packed + q + 1) * LANES]
                    for q in range(packed)
                    for level in range(levels)
                ],
                0,
            )
            at = pl.multiple_of((i * groups + g) * LANES, LANES)
            by_cell[pl.ds(at, LANES), :] = stack.T
        return 0

    lax.fori_loop(0, rows, turn, 0)
    place_copy.wait()

    def pick(b, _):
        for c in range(block_cells):
            picked[pl.ds(c, 1), :] = by_cell[pl.ds(places_ref[b, c], 1), :]
        turned = picked[...].T
        cell = jnp.broadcast_to(cells_ref[pl.ds(b, 1), :], (recv, block_cells))
        which = lax.rem(lax.div(cell, LANES), packed)
        for level in range(levels):
            value = turned[level * recv : (level + 1) * recv]
            for q in range(1, packed):
                at = (q * levels + level) * recv
                value = jnp.where(which == q, turned[at : at + recv], value)
            samples_ref[b, :, level * block_cells : (level + 1) * block_cells] = value
        return 0

    lax.fori_loop(0, blocks, pick, 0)
    for store in stores:
        store.wait()


def run_samples(cells, field):
    levels, rows, recv, width = field.shape
    blocks, block_cells = cells.shape
    packed = LANES // (levels * recv)
    vmem = pl.BlockSpec(memory_space=pltpu.VMEM)
    hbm = pl.BlockSpec(memory_space=pl.ANY)
    return pl.pallas_call(
        sample_kernel,
        out_shape=(
            jax.ShapeDtypeStruct((recv, levels, rows, width), jnp.float32),
            jax.ShapeDtypeStruct((blocks, recv, levels * block_cells), jnp.float32),
        ),
        in_specs=[hbm, hbm],
        out_specs=(hbm, vmem),
        scratch_shapes=[
            pltpu.VMEM(cells.shape, jnp.int32),
            pltpu.VMEM(field.shape, jnp.float32),
            pltpu.VMEM((recv, levels, rows, width), jnp.float32),
            pltpu.VMEM((rows * width // packed, LANES), jnp.float32),
            pltpu.VMEM((block_cells, LANES), jnp.float32),
            pltpu.VMEM(cells.shape, jnp.int32),
            pltpu.SMEM(cells.shape, jnp.int32),
            pltpu.SemaphoreType.DMA,
            pltpu.SemaphoreType.DMA,
            pltpu.SemaphoreType.DMA,
            pltpu.SemaphoreType.DMA((recv,)),
        ],
        compiler_params=pltpu.CompilerParams(vmem_limit_bytes=VMEM_LIMIT),
        name="release_samples",
    )(cells, field)


def contract_kernel(samples_ref, profiles_ref, out_ref):
    batches, own, recv, depth = samples_ref.shape
    for b in range(own):
        left = samples_ref[:, b].reshape(batches * recv, depth)
        out_ref[b] = jnp.dot(
            left, profiles_ref[b], precision=lax.Precision.HIGHEST,
            preferred_element_type=jnp.float32,
        )


def run_contract(gathered, profiles):
    batches, strips, own, recv, depth = gathered.shape
    scenarios = profiles.shape[-1]
    return pl.pallas_call(
        contract_kernel,
        grid=(strips,),
        out_shape=jax.ShapeDtypeStruct((strips, own, batches * recv, scenarios), jnp.float32),
        in_specs=[
            pl.BlockSpec((batches, None, own, recv, depth), lambda s: (0, s, 0, 0, 0)),
            pl.BlockSpec((None, own, depth, scenarios), lambda s: (s, 0, 0, 0)),
        ],
        out_specs=pl.BlockSpec((None, own, batches * recv, scenarios), lambda s: (s, 0, 0, 0)),
        compiler_params=pltpu.CompilerParams(vmem_limit_bytes=VMEM_LIMIT),
        name="scenario_response",
    )(gathered, profiles)


def on_device(
    adjoint_end, currents, plan, water_mask, mixing, decay, obs_weight, release_cells, profiles
):
    batches = lax.axis_size("rcpt")
    strips = lax.axis_size("space")
    stepped = run_steps(
        batches, strips, plan, decay, obs_weight, water_mask, mixing, adjoint_end, currents
    )
    field, samples = run_samples(release_cells[0], stepped)
    gathered = lax.all_to_all(samples, ("rcpt", "space"), split_axis=0, concat_axis=0, tiled=True)
    own = samples.shape[0] // (batches * strips)
    gathered = gathered.reshape((batches, strips, own) + samples.shape[1:])
    return (field, run_contract(gathered, profiles))


def solution(mesh):
    placed = (
        P("rcpt", None, "space", None),
        P("rcpt", None, None, "space", None),
        P(),
        P("space", None),
        P(None, "space", None),
        P("rcpt"),
        P(None, "rcpt"),
        P("space", None, None),
        P(None, ("rcpt", "space"), None, None),
    )
    return jax.shard_map(
        on_device,
        mesh=mesh,
        in_specs=placed,
        out_specs=(P("rcpt", None, "space", None), P(None, ("rcpt", "space"), None, None)),
        check_vma=False,
    )
```

```python
import functools

import jax
import jax.numpy as jnp
from jax import lax
from jax.experimental import pallas as pl
from jax.experimental.pallas import tpu as pltpu
from jax.sharding import PartitionSpec as P

HOURS = 4
LANES = 128
SUBROWS = 16
MESH = pl.DeviceIdType.MESH
VMEM_LIMIT = 63 * 1024 * 1024

diffusion_number = 0.08


def steps_kernel(
    batches, strips,
    plan_hbm, decay_hbm, obs_hbm, water_hbm, mix_hbm, adj_hbm, cur_hbm,
    out_hbm,
    plan_ref, decay_ref, obs_ref, water_ref, mix_ref,
    cur_parts, raw, fa, fb, src, halo, water_halo, gate, weight,
    cur_send, cur_recv, cur_own, halo_send, halo_recv, wat_send, wat_recv, in_sem, arg_sem, out_sem,
):
    recv, levels, rows, width = adj_hbm.shape
    slots = cur_hbm.shape[0]
    me = lax.axis_index("rcpt")
    strip = lax.axis_index("space")
    has_up = strip > 0
    has_down = strip < strips - 1

    barrier = pltpu.get_barrier_semaphore()
    for d in range(1, batches):
        pl.semaphore_signal(
            barrier, inc=1, device_id={"rcpt": lax.rem(me + d, batches)}, device_id_type=MESH
        )

    @pl.when(has_up)
    def _():
        pl.semaphore_signal(barrier, inc=1, device_id={"space": strip - 1}, device_id_type=MESH)

    @pl.when(has_down)
    def _():
        pl.semaphore_signal(barrier, inc=1, device_id={"space": strip + 1}, device_id_type=MESH)

    loads = [
        pltpu.make_async_copy(adj_hbm.at[r], raw.at[r], in_sem.at[r]) for r in range(recv)
    ]
    for load in loads:
        load.start()
    pairs = (
        (water_hbm, water_ref), (mix_hbm, mix_ref), (plan_hbm, plan_ref),
        (decay_hbm, decay_ref), (obs_hbm, obs_ref),
    )
    args = [
        pltpu.make_async_copy(there, here, arg_sem.at[k]) for k, (there, here) in enumerate(pairs)
    ]
    for arg in args:
        arg.start()
    parts = len(cur_parts)
    part_rows = rows // parts

    def slots_of(owner, part, component=None):
        at = pl.ds(owner * slots, slots)
        return cur_parts[part].at[at] if component is None else cur_parts[part].at[at, component]

    def stored(part):
        return cur_hbm.at[:, :, :, pl.ds(part * part_rows, part_rows)]

    own_copies = [
        pltpu.make_async_copy(stored(part), slots_of(me, part), cur_own.at[part])
        for part in range(parts)
    ]
    for copy in own_copies:
        copy.start()

    peers = batches - 1 + has_up.astype(jnp.int32) + has_down.astype(jnp.int32)
    pl.semaphore_wait(barrier, peers)

    def send(part, k, source, target, peer):
        return pltpu.make_async_remote_copy(
            src_ref=source, dst_ref=target,
            send_sem=cur_send.at[part, k], recv_sem=cur_recv.at[part, k],
            device_id={"rcpt": peer}, device_id_type=MESH,
        )

    square = batches == 4
    if square:
        side = me + 1 - 2 * lax.rem(me, 2)
        other = lax.rem(me + 2, batches)
        partners = (side, other)
    else:
        partners = tuple(lax.rem(me + d, batches) for d in range(1, batches))
    spread = [
        [
            send(
                part, k, stored(part), slots_of(me, part), peer,
            )
            for k, peer in enumerate(partners)
        ]
        for part in range(parts)
    ]
    passed = []
    if square:
        passed = [
            [
                send(part, 2, slots_of(other, part, 0), slots_of(other, part, 0), side),
                send(part, 3, slots_of(side, part, 1), slots_of(side, part, 1), other),
            ]
            for part in range(parts)
        ]
    for copies in spread:
        for copy in copies:
            copy.start()

    def pass_on(part):
        if square:
            spread[part][1].wait_recv()
            passed[part][0].start()
            spread[part][0].wait_recv()
            passed[part][1].start()

    def arrived(part):
        if square:
            for copy in passed[part]:
                copy.wait_recv()
        else:
            for copy in spread[part]:
                copy.wait_recv()

    def water_copies():
        up = pltpu.make_async_remote_copy(
            src_ref=water_hbm.at[pl.ds(0, 8)], dst_ref=water_halo.at[1],
            send_sem=wat_send.at[0], recv_sem=wat_recv.at[0],
            device_id={"space": strip - 1}, device_id_type=MESH,
        )
        down = pltpu.make_async_remote_copy(
            src_ref=water_hbm.at[pl.ds(rows - 8, 8)], dst_ref=water_halo.at[0],
            send_sem=wat_send.at[1], recv_sem=wat_recv.at[1],
            device_id={"space": strip + 1}, device_id_type=MESH,
        )
        return up, down

    def halo_copies(step, field):
        up = pltpu.make_async_remote_copy(
            src_ref=field.at[:, 0], dst_ref=halo.at[step, 1],
            send_sem=halo_send.at[step, 0], recv_sem=halo_recv.at[step, 0],
            device_id={"space": strip - 1}, device_id_type=MESH,
        )
        down = pltpu.make_async_remote_copy(
            src_ref=field.at[:, rows - 1], dst_ref=halo.at[step, 0],
            send_sem=halo_send.at[step, 1], recv_sem=halo_recv.at[step, 1],
            device_id={"space": strip + 1}, device_id_type=MESH,
        )
        return up, down

    def start(copies):
        up, down = copies

        @pl.when(has_up)
        def _():
            up.start()

        @pl.when(has_down)
        def _():
            down.start()

    def finish(copies):
        up, down = copies

        @pl.when(has_up)
        def _():
            up.wait_send()
            down.wait_recv()

        @pl.when(has_down)
        def _():
            down.wait_send()
            up.wait_recv()

    water_pair = water_copies()
    start(water_pair)

    for load in loads:
        load.wait()

    def arrange(t, _):
        for level in range(levels):
            block = raw[:, level, pl.ds(pl.multiple_of(t * 8, 8), 8), :]
            fa[level, pl.ds(t * 8, 8)] = jnp.swapaxes(block, 0, 1)
        return 0

    lax.fori_loop(0, rows // 8, arrange, 0)
    pair = halo_copies(0, fa)
    start(pair)

    @pl.when(jnp.logical_not(has_up))
    def _():
        water_halo[0] = jnp.zeros_like(water_halo[0])
        for step in range(HOURS):
            halo[step, 0] = jnp.zeros_like(halo[step, 0])

    @pl.when(jnp.logical_not(has_down))
    def _():
        water_halo[1] = jnp.zeros_like(water_halo[1])
        for step in range(HOURS):
            halo[step, 1] = jnp.zeros_like(halo[step, 1])

    for arg in args:
        arg.wait()
    finish(water_pair)
    inner = water_ref[...].astype(jnp.float32)
    above = water_halo[0, 7:8, :].astype(jnp.float32)
    below = water_halo[1, 0:1, :].astype(jnp.float32)
    row_at = lax.broadcasted_iota(jnp.int32, (rows, width), 0)
    col_at = lax.broadcasted_iota(jnp.int32, (rows, width), 1)
    up_water = jnp.where(row_at == 0, above, pltpu.roll(inner, 1, 0))
    down_water = jnp.where(row_at == rows - 1, below, pltpu.roll(inner, rows - 1, 0))
    left_water = jnp.where(col_at == 0, 0.0, pltpu.roll(inner, 1, 1))
    right_water = jnp.where(col_at == width - 1, 0.0, pltpu.roll(inner, width - 1, 1))
    gate[0] = inner
    gate[1] = inner * up_water
    gate[2] = inner * down_water
    gate[3] = inner * left_water
    gate[4] = inner * right_water

    def make_source(i, _):
        here = gate[0, pl.ds(i, 1), :]
        for level in range(levels):
            src[level, i] = fa[level, i] * here
        return 0

    lax.fori_loop(0, rows, make_source, 0)

    sub = lax.broadcasted_iota(jnp.int32, (recv, LANES), 0)

    def per_receptor(read):
        value = jnp.zeros((recv, LANES), jnp.float32)
        for r in range(recv):
            value = jnp.where(sub == r, read(r), value)
        return jnp.concatenate([value] * (width // LANES), 1)

    keep = per_receptor(lambda r: 1.0 - decay_ref[r])

    def make_weights(part):
        buffer = cur_parts[part]

        def tile(t, _):
            held = pl.ds(pl.multiple_of(t * SUBROWS, SUBROWS), SUBROWS)
            at = pl.ds(pl.multiple_of(part * part_rows + t * SUBROWS, SUBROWS), SUBROWS)
            for hour in range(HOURS):
                slot = plan_ref[hour]
                for level in range(levels):
                    along = buffer[slot, 0, level, held, :].astype(jnp.float32)
                    across = buffer[slot, 1, level, held, :].astype(jnp.float32)
                    up = (jnp.maximum(-along, 0.0) + diffusion_number) * gate[1, at, :]
                    down = (jnp.maximum(along, 0.0) + diffusion_number) * gate[2, at, :]
                    left = (jnp.maximum(-across, 0.0) + diffusion_number) * gate[3, at, :]
                    right = (jnp.maximum(across, 0.0) + diffusion_number) * gate[4, at, :]
                    middle = gate[0, at, :] - ((up + down) + (left + right))
                    for k, value in enumerate((middle, up, down, left, right)):
                        weight[hour, k, level, at, :] = value
            return 0

        lax.fori_loop(0, part_rows // SUBROWS, tile, 0)

    def do_row(hour, fin, fout, i, upper, lower, obs):
        at = pl.ds(i, 1)

        def moved_at(level):
            center = fin[level, i]
            out = center * weight[hour, 0, level, at, :]
            out = out + upper(level) * weight[hour, 1, level, at, :]
            out = out + lower(level) * weight[hour, 2, level, at, :]
            out = out + pltpu.roll(center, 1, 1) * weight[hour, 3, level, at, :]
            return out + pltpu.roll(center, width - 1, 1) * weight[hour, 4, level, at, :]

        moved = moved_at(0)
        flux = None
        for level in range(levels):
            mixed = moved
            if flux is not None:
                mixed = mixed - flux
            if level < levels - 1:
                following = moved_at(level + 1)
                flux = mix_ref[level, at, :] * (following - moved)
                mixed = mixed + flux
                moved = following
            fout[level, i] = keep * mixed + obs * src[level, i]

    seen = [per_receptor(lambda r, h=h: obs_ref[h, r]) for h in range(HOURS)]

    def buffers(step):
        return (fa, fb) if step % 2 == 0 else (fb, fa)

    def span(step, low, high):
        hour = HOURS - 1 - step
        fin, fout = buffers(step)

        def body(i, _):
            do_row(
                hour, fin, fout, i,
                lambda level: fin[level, i - 1], lambda level: fin[level, i + 1], seen[hour],
            )
            return 0

        if low < high:
            lax.fori_loop(low, high, body, 0)

    def first_row(step):
        hour = HOURS - 1 - step
        fin, fout = buffers(step)
        do_row(
            hour, fin, fout, 0,
            lambda level: halo[step, 0, level], lambda level: fin[level, 1], seen[hour],
        )

    def last_row(step):
        hour = HOURS - 1 - step
        fin, fout = buffers(step)
        do_row(
            hour, fin, fout, rows - 1,
            lambda level: fin[level, rows - 2], lambda level: halo[step, 1, level], seen[hour],
        )

    for copy in own_copies:
        copy.wait()
    pass_on(0)
    for part in range(parts):
        arrived(part)
        if part < parts - 1:
            make_weights(part)
            for step in range(HOURS):
                span(step, step + 1, part_rows - 1 - step)
                if step == 0:
                    pass_on(part + 1)
    make_weights(parts - 1)
    early = parts > 1
    for step in range(HOURS):
        finish(pair)
        first_row(step)
        last_row(step)
        if step < HOURS - 1:
            pair = halo_copies(step + 1, buffers(step)[1])
            start(pair)
        low = max(part_rows - 1 - step, step + 1) if early else 1
        if early:
            span(step, 1, step + 1)
        if step < HOURS - 1:
            span(step, low, rows - 1)
    result = buffers(HOURS - 1)[1]
    leaving = []
    for t in range(rows // 8):
        span(HOURS - 1, max(low, t * 8), min(rows - 1, t * 8 + 8))
        piece = pl.ds(t * 8, 8)
        leaving.append(
            pltpu.make_async_copy(result.at[:, piece], out_hbm.at[:, piece], out_sem.at[t])
        )
        leaving[-1].start()
    for copy in leaving:
        copy.wait()
    for copies in spread + passed:
        for copy in copies:
            copy.wait_send()


def run_steps(batches, strips, plan, decay, obs_weight, water, mixing, adjoint_end, currents):
    recv, levels, rows, width = adjoint_end.shape
    field = (levels, rows, recv, width)
    slots = currents.shape[0]
    parts = 2 if rows % (2 * SUBROWS) == 0 else 1
    hbm = pl.BlockSpec(memory_space=pl.ANY)
    dma = pltpu.SemaphoreType.DMA
    return pl.pallas_call(
        functools.partial(steps_kernel, batches, strips),
        out_shape=jax.ShapeDtypeStruct(field, jnp.float32),
        in_specs=[hbm] * 7,
        out_specs=hbm,
        scratch_shapes=[
            pltpu.SMEM(plan.shape, jnp.int32),
            pltpu.SMEM(decay.shape, jnp.float32),
            pltpu.SMEM(obs_weight.shape, jnp.float32),
            pltpu.VMEM(water.shape, jnp.int32),
            pltpu.VMEM(mixing.shape, jnp.float32),
            [
                pltpu.VMEM(
                    (batches * slots, 2, levels, rows // parts, width), currents.dtype
                )
            ]
            * parts,
            pltpu.VMEM(adjoint_end.shape, jnp.float32),
            pltpu.VMEM(field, jnp.float32),
            pltpu.VMEM(field, jnp.float32),
            pltpu.VMEM(field, jnp.float32),
            pltpu.VMEM((HOURS, 2, levels, recv, width), jnp.float32),
            pltpu.VMEM((2, 8, width), jnp.int32),
            pltpu.VMEM((5, rows, width), jnp.float32),
            pltpu.VMEM((HOURS, 5, levels, rows, width), jnp.float32),
            dma((parts, max(batches - 1, 4))),
            dma((parts, max(batches - 1, 4))),
            dma((parts,)),
            dma((HOURS, 2)),
            dma((HOURS, 2)),
            dma((2,)),
            dma((2,)),
            dma((recv,)),
            dma((5,)),
            dma((rows // 8,)),
        ],
        compiler_params=pltpu.CompilerParams(
            collective_id=0, has_side_effects=True, vmem_limit_bytes=VMEM_LIMIT
        ),
        name="transport_steps",
    )(plan, decay, obs_weight, water, mixing, adjoint_end, currents)


def turn_kernel(field_hbm, out_hbm, by_cell_hbm, field, native, by_cell, in_sem, out_sem, cell_sem):
    levels, rows, recv, width = field.shape
    tiles = width // LANES
    packed = LANES // (levels * recv)
    groups = tiles // packed
    pieces = [pl.ds(t * 8, 8) for t in range(rows // 8)]
    loads = [
        pltpu.make_async_copy(field_hbm.at[:, piece], field.at[:, piece], in_sem.at[t])
        for t, piece in enumerate(pieces)
    ]
    for load in loads:
        load.start()

    def turn(i, _):
        for g in range(groups):
            stack = jnp.concatenate(
                [
                    field[level, i, :, (g * packed + q) * LANES : (g * packed + q + 1) * LANES]
                    for q in range(packed)
                    for level in range(levels)
                ],
                0,
            )
            at = pl.multiple_of((i * groups + g) * LANES, LANES)
            by_cell[pl.ds(at, LANES), :] = stack.T
        return 0

    leaving = []
    for t, piece in enumerate(pieces):
        loads[t].wait()
        for level in range(levels):
            native[:, level, piece, :] = jnp.swapaxes(field[level, piece], 0, 1)
        leaving.append(
            pltpu.make_async_copy(
                native.at[:, :, piece], out_hbm.at[:, :, piece], out_sem.at[t]
            )
        )
        leaving[-1].start()
        lax.fori_loop(t * 8, t * 8 + 8, turn, 0)
        held = pl.ds(t * 8 * groups * LANES, 8 * groups * LANES)
        leaving.append(
            pltpu.make_async_copy(by_cell.at[held], by_cell_hbm.at[held], cell_sem.at[t])
        )
        leaving[-1].start()
    for copy in leaving:
        copy.wait()


def run_turn(field):
    levels, rows, recv, width = field.shape
    packed = LANES // (levels * recv)
    by_cell = (rows * width // packed, LANES)
    hbm = pl.BlockSpec(memory_space=pl.ANY)
    return pl.pallas_call(
        turn_kernel,
        out_shape=(
            jax.ShapeDtypeStruct((recv, levels, rows, width), jnp.float32),
            jax.ShapeDtypeStruct(by_cell, jnp.float32),
        ),
        in_specs=[hbm],
        out_specs=(hbm, hbm),
        scratch_shapes=[
            pltpu.VMEM(field.shape, jnp.float32),
            pltpu.VMEM((recv, levels, rows, width), jnp.float32),
            pltpu.VMEM(by_cell, jnp.float32),
            pltpu.SemaphoreType.DMA((rows // 8,)),
            pltpu.SemaphoreType.DMA((rows // 8,)),
            pltpu.SemaphoreType.DMA((rows // 8,)),
        ],
        compiler_params=pltpu.CompilerParams(vmem_limit_bytes=VMEM_LIMIT),
        name="cell_major",
    )(field)


def response_kernel(
    batches, strips, recv, levels,
    cells_hbm, by_cell_hbm, profiles_hbm, out_ref,
    by_cell, profiles_ref, cells_ref, places, places_ref, picked, sending, landed,
    cell_sem, place_sem, load_sem, send_sem, recv_sem,
):
    blocks, block_cells = cells_ref.shape
    own = blocks // (batches * strips)
    packed = LANES // (levels * recv)
    batch = lax.axis_index("rcpt")
    strip = lax.axis_index("space")
    cell_load = pltpu.make_async_copy(cells_hbm, cells_ref, cell_sem)
    cell_load.start()
    load = pltpu.make_async_copy(by_cell_hbm, by_cell, load_sem.at[0])
    load.start()
    profile_load = pltpu.make_async_copy(profiles_hbm, profiles_ref, load_sem.at[1])
    profile_load.start()

    barrier = pltpu.get_barrier_semaphore()

    def peer(j, i):
        return {"rcpt": lax.rem(batch + i, batches), "space": lax.rem(strip + j, strips)}

    for i in range(1, batches):
        pl.semaphore_signal(barrier, inc=1, device_id=peer(0, i), device_id_type=MESH)

    def greet(j, _):
        for i in range(batches):
            pl.semaphore_signal(barrier, inc=1, device_id=peer(j, i), device_id_type=MESH)
        return 0

    lax.fori_loop(1, strips, greet, 0)

    cell_load.wait()
    cells = cells_ref[...]
    places[...] = lax.div(lax.div(cells, LANES), packed) * LANES + lax.rem(cells, LANES)
    place_copy = pltpu.make_async_copy(places, places_ref, place_sem)
    place_copy.start()
    place_copy.wait()
    load.wait()

    def pick(j, i, put):
        target = peer(j, i)
        first = (target["rcpt"] * strips + target["space"]) * own
        for k in range(own):
            b = first + k
            for c in range(block_cells):
                picked[pl.ds(c, 1), :] = by_cell[pl.ds(places_ref[b, c], 1), :]
            turned = picked[...].T
            cell = jnp.broadcast_to(cells_ref[pl.ds(b, 1), :], (recv, block_cells))
            which = lax.rem(lax.div(cell, LANES), packed)
            for level in range(levels):
                value = turned[level * recv : (level + 1) * recv]
                for q in range(1, packed):
                    at = (q * levels + level) * recv
                    value = jnp.where(which == q, turned[at : at + recv], value)
                put(k, slice(level * block_cells, (level + 1) * block_cells), value)

    def copy_to(j, i):
        return pltpu.make_async_remote_copy(
            src_ref=sending.at[j, i], dst_ref=landed.at[strip, batch],
            send_sem=send_sem.at[j, i], recv_sem=recv_sem.at[j, i],
            device_id=peer(j, i), device_id_type=MESH,
        )

    def sample(j, i):
        def put(k, at, value):
            sending[j, i, k, :, at] = value

        pick(j, i, put)
        copy_to(j, i).start()

    pl.semaphore_wait(barrier, batches * strips - 1)

    def sample_strip(j, _):
        def one(i, _):
            sample(j, i)
            return 0

        lax.fori_loop(0, batches, one, 0)
        return 0

    lax.fori_loop(1, strips, sample_strip, 0)

    def sample_own_strip(i, _):
        sample(0, i)
        return 0

    lax.fori_loop(1, batches, sample_own_strip, 0)

    def put_own(k, at, value):
        landed[strip, batch, k, :, at] = value

    pick(0, 0, put_own)
    profile_load.wait()

    def contract(s):
        for k in range(own):
            left = landed[s, :, k].reshape(batches * recv, levels * block_cells)
            out_ref[s, k] = jnp.dot(
                left, profiles_ref[s, k], precision=lax.Precision.HIGHEST,
                preferred_element_type=jnp.float32,
            )

    def receive(j, _):
        for i in range(batches):
            copy_to(j, i).wait_recv()
        contract(lax.rem(strip + strips - j, strips))
        return 0

    lax.fori_loop(1, strips, receive, 0)
    for i in range(1, batches):
        copy_to(0, i).wait_recv()
    contract(strip)

    def sent(j, _):
        for i in range(batches):
            copy_to(j, i).wait_send()
        return 0

    lax.fori_loop(1, strips, sent, 0)
    for i in range(1, batches):
        copy_to(0, i).wait_send()


def run_response(batches, strips, recv, levels, cells, by_cell, profiles):
    blocks, block_cells = cells.shape
    own = blocks // (batches * strips)
    depth, scenarios = profiles.shape[-2:]
    vmem = pl.BlockSpec(memory_space=pltpu.VMEM)
    dma = pltpu.SemaphoreType.DMA
    return pl.pallas_call(
        functools.partial(response_kernel, batches, strips, recv, levels),
        out_shape=jax.ShapeDtypeStruct((strips, own, batches * recv, scenarios), jnp.float32),
        in_specs=[pl.BlockSpec(memory_space=pl.ANY)] * 3,
        out_specs=vmem,
        scratch_shapes=[
            pltpu.VMEM(by_cell.shape, jnp.float32),
            pltpu.VMEM(profiles.shape, jnp.float32),
            pltpu.VMEM(cells.shape, jnp.int32),
            pltpu.VMEM(cells.shape, jnp.int32),
            pltpu.SMEM(cells.shape, jnp.int32),
            pltpu.VMEM((block_cells, LANES), jnp.float32),
            pltpu.VMEM((strips, batches, own, recv, depth), jnp.float32),
            pltpu.VMEM((strips, batches, own, recv, depth), jnp.float32),
            dma,
            dma,
            dma((2,)),
            dma((strips, batches)),
            dma((strips, batches)),
        ],
        compiler_params=pltpu.CompilerParams(
            collective_id=1, has_side_effects=True, vmem_limit_bytes=VMEM_LIMIT
        ),
        name="release_response",
    )(cells, by_cell, profiles)


def on_device(
    adjoint_end, currents, plan, water_mask, mixing, decay, obs_weight, release_cells, profiles
):
    batches = lax.axis_size("rcpt")
    strips = lax.axis_size("space")
    stepped = run_steps(
        batches, strips, plan, decay, obs_weight, water_mask, mixing, adjoint_end, currents
    )
    field, by_cell = run_turn(stepped)
    recv, levels = adjoint_end.shape[:2]
    response = run_response(
        batches, strips, recv, levels, release_cells[0], by_cell, profiles
    )
    return (field, response)


def solution(mesh):
    placed = (
        P("rcpt", None, "space", None),
        P("rcpt", None, None, "space", None),
        P(),
        P("space", None),
        P(None, "space", None),
        P("rcpt"),
        P(None, "rcpt"),
        P("space", None, None),
        P(None, ("rcpt", "space"), None, None),
    )
    return jax.shard_map(
        on_device,
        mesh=mesh,
        in_specs=placed,
        out_specs=(P("rcpt", None, "space", None), P(None, ("rcpt", "space"), None, None)),
        check_vma=False,
    )
```

```python
import functools

import jax
import jax.numpy as jnp
from jax import lax
from jax.experimental import pallas as pl
from jax.experimental.pallas import tpu as pltpu
from jax.sharding import PartitionSpec as P

HOURS = 4
LANES = 128
SUBROWS = 16
CHUNK = 256
MESH = pl.DeviceIdType.MESH
VMEM_LIMIT = 63 * 1024 * 1024

diffusion_number = 0.08


def steps_kernel(
    batches, strips,
    plan_hbm, decay_hbm, obs_hbm, water_hbm, mix_hbm, adj_hbm, cur_hbm,
    out_hbm,
    plan_ref, decay_ref, obs_ref, water_ref, mix_ref,
    cur_parts, raw, fa, fb, src, halo, water_halo, gate, weight,
    cur_send, cur_recv, cur_own, halo_send, halo_recv, wat_send, wat_recv, in_sem, arg_sem, out_sem,
):
    recv, levels, rows, width = adj_hbm.shape
    slots = cur_hbm.shape[0]
    me = lax.axis_index("rcpt")
    strip = lax.axis_index("space")
    has_up = strip > 0
    has_down = strip < strips - 1

    barrier = pltpu.get_barrier_semaphore()
    for d in range(1, batches):
        pl.semaphore_signal(
            barrier, inc=1, device_id={"rcpt": lax.rem(me + d, batches)}, device_id_type=MESH
        )

    @pl.when(has_up)
    def _():
        pl.semaphore_signal(barrier, inc=1, device_id={"space": strip - 1}, device_id_type=MESH)

    @pl.when(has_down)
    def _():
        pl.semaphore_signal(barrier, inc=1, device_id={"space": strip + 1}, device_id_type=MESH)

    loads = [
        pltpu.make_async_copy(adj_hbm.at[r], raw.at[r], in_sem.at[r]) for r in range(recv)
    ]
    for load in loads:
        load.start()
    pairs = (
        (water_hbm, water_ref), (mix_hbm, mix_ref), (plan_hbm, plan_ref),
        (decay_hbm, decay_ref), (obs_hbm, obs_ref),
    )
    args = [
        pltpu.make_async_copy(there, here, arg_sem.at[k]) for k, (there, here) in enumerate(pairs)
    ]
    for arg in args:
        arg.start()
    parts = len(cur_parts)
    part_rows = rows // parts

    def slots_of(owner, part, component=None):
        at = pl.ds(owner * slots, slots)
        return cur_parts[part].at[at] if component is None else cur_parts[part].at[at, component]

    def stored(part):
        return cur_hbm.at[:, :, :, pl.ds(part * part_rows, part_rows)]

    own_copies = [
        pltpu.make_async_copy(stored(part), slots_of(me, part), cur_own.at[part])
        for part in range(parts)
    ]
    for copy in own_copies:
        copy.start()

    peers = batches - 1 + has_up.astype(jnp.int32) + has_down.astype(jnp.int32)
    pl.semaphore_wait(barrier, peers)

    def send(part, k, source, target, peer):
        return pltpu.make_async_remote_copy(
            src_ref=source, dst_ref=target,
            send_sem=cur_send.at[part, k], recv_sem=cur_recv.at[part, k],
            device_id={"rcpt": peer}, device_id_type=MESH,
        )

    square = batches == 4
    if square:
        side = me + 1 - 2 * lax.rem(me, 2)
        other = lax.rem(me + 2, batches)
        partners = (side, other)
    else:
        partners = tuple(lax.rem(me + d, batches) for d in range(1, batches))
    spread = [
        [
            send(
                part, k, stored(part), slots_of(me, part), peer,
            )
            for k, peer in enumerate(partners)
        ]
        for part in range(parts)
    ]
    passed = []
    if square:
        passed = [
            [
                send(part, 2, slots_of(other, part, 0), slots_of(other, part, 0), side),
                send(part, 3, slots_of(side, part, 1), slots_of(side, part, 1), other),
            ]
            for part in range(parts)
        ]
    for copy in spread[0]:
        copy.start()

    def pass_on(part):
        if square:
            spread[part][1].wait_recv()
            passed[part][0].start()
            spread[part][0].wait_recv()
            passed[part][1].start()

    def arrived(part):
        if square:
            for copy in passed[part]:
                copy.wait_recv()
        else:
            for copy in spread[part]:
                copy.wait_recv()

    def water_copies():
        up = pltpu.make_async_remote_copy(
            src_ref=water_hbm.at[pl.ds(0, 8)], dst_ref=water_halo.at[1],
            send_sem=wat_send.at[0], recv_sem=wat_recv.at[0],
            device_id={"space": strip - 1}, device_id_type=MESH,
        )
        down = pltpu.make_async_remote_copy(
            src_ref=water_hbm.at[pl.ds(rows - 8, 8)], dst_ref=water_halo.at[0],
            send_sem=wat_send.at[1], recv_sem=wat_recv.at[1],
            device_id={"space": strip + 1}, device_id_type=MESH,
        )
        return up, down

    def halo_copies(step, field):
        up = pltpu.make_async_remote_copy(
            src_ref=field.at[:, 0], dst_ref=halo.at[step, 1],
            send_sem=halo_send.at[step, 0], recv_sem=halo_recv.at[step, 0],
            device_id={"space": strip - 1}, device_id_type=MESH,
        )
        down = pltpu.make_async_remote_copy(
            src_ref=field.at[:, rows - 1], dst_ref=halo.at[step, 0],
            send_sem=halo_send.at[step, 1], recv_sem=halo_recv.at[step, 1],
            device_id={"space": strip + 1}, device_id_type=MESH,
        )
        return up, down

    def start(copies):
        up, down = copies

        @pl.when(has_up)
        def _():
            up.start()

        @pl.when(has_down)
        def _():
            down.start()

    def finish(copies):
        up, down = copies

        @pl.when(has_up)
        def _():
            up.wait_send()
            down.wait_recv()

        @pl.when(has_down)
        def _():
            down.wait_send()
            up.wait_recv()

    water_pair = water_copies()
    start(water_pair)

    for load in loads:
        load.wait()

    def arrange(t, _):
        for level in range(levels):
            block = raw[:, level, pl.ds(pl.multiple_of(t * 8, 8), 8), :]
            fa[level, pl.ds(t * 8, 8)] = jnp.swapaxes(block, 0, 1)
        return 0

    lax.fori_loop(0, rows // 8, arrange, 0)
    pair = halo_copies(0, fa)
    start(pair)

    @pl.when(jnp.logical_not(has_up))
    def _():
        water_halo[0] = jnp.zeros_like(water_halo[0])
        for step in range(HOURS):
            halo[step, 0] = jnp.zeros_like(halo[step, 0])

    @pl.when(jnp.logical_not(has_down))
    def _():
        water_halo[1] = jnp.zeros_like(water_halo[1])
        for step in range(HOURS):
            halo[step, 1] = jnp.zeros_like(halo[step, 1])

    for arg in args:
        arg.wait()
    finish(water_pair)
    inner = water_ref[...].astype(jnp.float32)
    above = water_halo[0, 7:8, :].astype(jnp.float32)
    below = water_halo[1, 0:1, :].astype(jnp.float32)
    row_at = lax.broadcasted_iota(jnp.int32, (rows, width), 0)
    col_at = lax.broadcasted_iota(jnp.int32, (rows, width), 1)
    up_water = jnp.where(row_at == 0, above, pltpu.roll(inner, 1, 0))
    down_water = jnp.where(row_at == rows - 1, below, pltpu.roll(inner, rows - 1, 0))
    left_water = jnp.where(col_at == 0, 0.0, pltpu.roll(inner, 1, 1))
    right_water = jnp.where(col_at == width - 1, 0.0, pltpu.roll(inner, width - 1, 1))
    gate[0] = inner
    gate[1] = inner * up_water
    gate[2] = inner * down_water
    gate[3] = inner * left_water
    gate[4] = inner * right_water

    def make_source(i, _):
        here = gate[0, pl.ds(i, 1), :]
        for level in range(levels):
            src[level, i] = fa[level, i] * here
        return 0

    lax.fori_loop(0, rows, make_source, 0)

    sub = lax.broadcasted_iota(jnp.int32, (recv, LANES), 0)

    def per_receptor(read):
        value = jnp.zeros((recv, LANES), jnp.float32)
        for r in range(recv):
            value = jnp.where(sub == r, read(r), value)
        return jnp.concatenate([value] * (min(CHUNK, width) // LANES), 1)

    keep = per_receptor(lambda r: 1.0 - decay_ref[r])

    def make_weights(part):
        buffer = cur_parts[part]

        def tile(t, _):
            held = pl.ds(pl.multiple_of(t * SUBROWS, SUBROWS), SUBROWS)
            at = pl.ds(pl.multiple_of(part * part_rows + t * SUBROWS, SUBROWS), SUBROWS)
            for hour in range(HOURS):
                slot = plan_ref[hour]
                for level in range(levels):
                    along = buffer[slot, 0, level, held, :].astype(jnp.float32)
                    across = buffer[slot, 1, level, held, :].astype(jnp.float32)
                    up = (jnp.maximum(-along, 0.0) + diffusion_number) * gate[1, at, :]
                    down = (jnp.maximum(along, 0.0) + diffusion_number) * gate[2, at, :]
                    left = (jnp.maximum(-across, 0.0) + diffusion_number) * gate[3, at, :]
                    right = (jnp.maximum(across, 0.0) + diffusion_number) * gate[4, at, :]
                    middle = gate[0, at, :] - ((up + down) + (left + right))
                    for k, value in enumerate((middle, up, down, left, right)):
                        weight[hour, k, level, at, :] = value
            return 0

        lax.fori_loop(0, part_rows // SUBROWS, tile, 0)

    chunk = min(CHUNK, width)

    def do_rows(hour, fin, fout, i, count, upper, lower, obs):
        for start in range(0, width, chunk):
            cols = slice(start, start + chunk)

            def beside(level, k, center):
                if start > 0:
                    wide = fin[level, i + k, :, start - LANES : start + chunk]
                    before = pltpu.roll(wide, 1, 1)[:, LANES:]
                else:
                    before = pltpu.roll(center, 1, 1)
                if start + chunk < width:
                    wide = fin[level, i + k, :, start : start + chunk + LANES]
                    after = pltpu.roll(wide, chunk + LANES - 1, 1)[:, :chunk]
                else:
                    after = pltpu.roll(center, chunk - 1, 1)
                return before, after

            def moved_at(level):
                lines = [upper(level, cols)]
                lines += [fin[level, i + k, :, cols] for k in range(count)]
                lines += [lower(level, cols)]
                found = []
                for k in range(count):
                    center = lines[k + 1]
                    before, after = beside(level, k, center)
                    factor = [weight[hour, n, level, pl.ds(i + k, 1), cols] for n in range(5)]
                    out = center * factor[0] + lines[k] * factor[1]
                    out = out + lines[k + 2] * factor[2]
                    found.append(out + before * factor[3] + after * factor[4])
                return found

            moved = moved_at(0)
            flux = None
            for level in range(levels):
                mixed = moved
                if flux is not None:
                    mixed = [m - f for m, f in zip(mixed, flux)]
                if level < levels - 1:
                    following = moved_at(level + 1)
                    flux = [
                        mix_ref[level, pl.ds(i + k, 1), cols] * (following[k] - moved[k])
                        for k in range(count)
                    ]
                    mixed = [m + f for m, f in zip(mixed, flux)]
                    moved = following
                for k in range(count):
                    fout[level, i + k, :, cols] = (
                        keep * mixed[k] + obs * src[level, i + k, :, cols]
                    )

    seen = [per_receptor(lambda r, h=h: obs_ref[h, r]) for h in range(HOURS)]

    def buffers(step):
        return (fa, fb) if step % 2 == 0 else (fb, fa)

    def span(step, low, high):
        hour = HOURS - 1 - step
        fin, fout = buffers(step)

        def some(i, count):
            do_rows(
                hour, fin, fout, i, count,
                lambda level, cols: fin[level, i - 1, :, cols],
                lambda level, cols: fin[level, i + count, :, cols],
                seen[hour],
            )

        def body(t, _):
            some(low + 2 * t, 2)
            return 0

        if high - low > 1:
            lax.fori_loop(0, (high - low) // 2, body, 0)
        if low < high and (high - low) % 2:
            some(high - 1, 1)

    def first_row(step):
        hour = HOURS - 1 - step
        fin, fout = buffers(step)
        do_rows(
            hour, fin, fout, 0, 1,
            lambda level, cols: halo[step, 0, level, :, cols],
            lambda level, cols: fin[level, 1, :, cols],
            seen[hour],
        )

    def last_row(step):
        hour = HOURS - 1 - step
        fin, fout = buffers(step)
        do_rows(
            hour, fin, fout, rows - 1, 1,
            lambda level, cols: fin[level, rows - 2, :, cols],
            lambda level, cols: halo[step, 1, level, :, cols],
            seen[hour],
        )

    for copy in own_copies:
        copy.wait()
    pass_on(0)
    for copies in spread[1:]:
        for copy in copies:
            copy.start()
    for part in range(parts):
        arrived(part)
        if part < parts - 1:
            make_weights(part)
            for step in range(HOURS):
                span(step, step + 1, part_rows - 1 - step)
                if step == 0:
                    pass_on(part + 1)
    make_weights(parts - 1)
    early = parts > 1
    for step in range(HOURS):
        finish(pair)
        first_row(step)
        last_row(step)
        if step < HOURS - 1:
            pair = halo_copies(step + 1, buffers(step)[1])
            start(pair)
        low = max(part_rows - 1 - step, step + 1) if early else 1
        if early:
            span(step, 1, step + 1)
        if step < HOURS - 1:
            span(step, low, rows - 1)
    result = buffers(HOURS - 1)[1]
    leaving = []
    for t in range(rows // 8):
        span(HOURS - 1, max(low, t * 8), min(rows - 1, t * 8 + 8))
        piece = pl.ds(t * 8, 8)
        leaving.append(
            pltpu.make_async_copy(result.at[:, piece], out_hbm.at[:, piece], out_sem.at[t])
        )
        leaving[-1].start()
    for copy in leaving:
        copy.wait()
    for copies in spread + passed:
        for copy in copies:
            copy.wait_send()


def run_steps(batches, strips, plan, decay, obs_weight, water, mixing, adjoint_end, currents):
    recv, levels, rows, width = adjoint_end.shape
    field = (levels, rows, recv, width)
    slots = currents.shape[0]
    parts = 2 if rows % (2 * SUBROWS) == 0 else 1
    hbm = pl.BlockSpec(memory_space=pl.ANY)
    dma = pltpu.SemaphoreType.DMA
    return pl.pallas_call(
        functools.partial(steps_kernel, batches, strips),
        out_shape=jax.ShapeDtypeStruct(field, jnp.float32),
        in_specs=[hbm] * 7,
        out_specs=hbm,
        scratch_shapes=[
            pltpu.SMEM(plan.shape, jnp.int32),
            pltpu.SMEM(decay.shape, jnp.float32),
            pltpu.SMEM(obs_weight.shape, jnp.float32),
            pltpu.VMEM(water.shape, jnp.int32),
            pltpu.VMEM(mixing.shape, jnp.float32),
            [
                pltpu.VMEM(
                    (batches * slots, 2, levels, rows // parts, width), currents.dtype
                )
            ]
            * parts,
            pltpu.VMEM(adjoint_end.shape, jnp.float32),
            pltpu.VMEM(field, jnp.float32),
            pltpu.VMEM(field, jnp.float32),
            pltpu.VMEM(field, jnp.float32),
            pltpu.VMEM((HOURS, 2, levels, recv, width), jnp.float32),
            pltpu.VMEM((2, 8, width), jnp.int32),
            pltpu.VMEM((5, rows, width), jnp.float32),
            pltpu.VMEM((HOURS, 5, levels, rows, width), jnp.float32),
            dma((parts, max(batches - 1, 4))),
            dma((parts, max(batches - 1, 4))),
            dma((parts,)),
            dma((HOURS, 2)),
            dma((HOURS, 2)),
            dma((2,)),
            dma((2,)),
            dma((recv,)),
            dma((5,)),
            dma((rows // 8,)),
        ],
        compiler_params=pltpu.CompilerParams(
            collective_id=0, has_side_effects=True, vmem_limit_bytes=VMEM_LIMIT
        ),
        name="transport_steps",
    )(plan, decay, obs_weight, water, mixing, adjoint_end, currents)


def turn_kernel(field_hbm, out_hbm, by_cell_hbm, field, native, by_cell, in_sem, out_sem, cell_sem):
    levels, rows, recv, width = field.shape
    tiles = width // LANES
    packed = LANES // (levels * recv)
    groups = tiles // packed
    pieces = [pl.ds(t * 8, 8) for t in range(rows // 8)]
    loads = [
        pltpu.make_async_copy(field_hbm.at[:, piece], field.at[:, piece], in_sem.at[t])
        for t, piece in enumerate(pieces)
    ]
    for load in loads:
        load.start()

    def turn(i, _):
        for g in range(groups):
            stack = jnp.concatenate(
                [
                    field[level, i, :, (g * packed + q) * LANES : (g * packed + q + 1) * LANES]
                    for q in range(packed)
                    for level in range(levels)
                ],
                0,
            )
            at = pl.multiple_of((i * groups + g) * LANES, LANES)
            by_cell[pl.ds(at, LANES), :] = stack.T
        return 0

    leaving = []
    for t, piece in enumerate(pieces):
        loads[t].wait()
        for level in range(levels):
            native[:, level, piece, :] = jnp.swapaxes(field[level, piece], 0, 1)
        leaving.append(
            pltpu.make_async_copy(
                native.at[:, :, piece], out_hbm.at[:, :, piece], out_sem.at[t]
            )
        )
        leaving[-1].start()
        lax.fori_loop(t * 8, t * 8 + 8, turn, 0)
        held = pl.ds(t * 8 * groups * LANES, 8 * groups * LANES)
        leaving.append(
            pltpu.make_async_copy(by_cell.at[held], by_cell_hbm.at[held], cell_sem.at[t])
        )
        leaving[-1].start()
    for copy in leaving:
        copy.wait()


def run_turn(field):
    levels, rows, recv, width = field.shape
    packed = LANES // (levels * recv)
    by_cell = (rows * width // packed, LANES)
    hbm = pl.BlockSpec(memory_space=pl.ANY)
    return pl.pallas_call(
        turn_kernel,
        out_shape=(
            jax.ShapeDtypeStruct((recv, levels, rows, width), jnp.float32),
            jax.ShapeDtypeStruct(by_cell, jnp.float32),
        ),
        in_specs=[hbm],
        out_specs=(hbm, hbm),
        scratch_shapes=[
            pltpu.VMEM(field.shape, jnp.float32),
            pltpu.VMEM((recv, levels, rows, width), jnp.float32),
            pltpu.VMEM(by_cell, jnp.float32),
            pltpu.SemaphoreType.DMA((rows // 8,)),
            pltpu.SemaphoreType.DMA((rows // 8,)),
            pltpu.SemaphoreType.DMA((rows // 8,)),
        ],
        compiler_params=pltpu.CompilerParams(vmem_limit_bytes=VMEM_LIMIT),
        name="cell_major",
    )(field)


def response_kernel(
    batches, strips, recv, levels,
    cells_hbm, by_cell_hbm, profiles_hbm, out_ref,
    by_cell, profiles_ref, cells_ref, places, places_ref, picked, sending, landed,
    cell_sem, place_sem, load_sem, send_sem, recv_sem,
):
    blocks, block_cells = cells_ref.shape
    own = blocks // (batches * strips)
    packed = LANES // (levels * recv)
    batch = lax.axis_index("rcpt")
    strip = lax.axis_index("space")
    cell_load = pltpu.make_async_copy(cells_hbm, cells_ref, cell_sem)
    cell_load.start()
    load = pltpu.make_async_copy(by_cell_hbm, by_cell, load_sem.at[0])
    load.start()
    profile_load = pltpu.make_async_copy(profiles_hbm, profiles_ref, load_sem.at[1])
    profile_load.start()

    barrier = pltpu.get_barrier_semaphore()

    def peer(j, i):
        return {"rcpt": lax.rem(batch + i, batches), "space": lax.rem(strip + j, strips)}

    for i in range(1, batches):
        pl.semaphore_signal(barrier, inc=1, device_id=peer(0, i), device_id_type=MESH)

    def greet(j, _):
        for i in range(batches):
            pl.semaphore_signal(barrier, inc=1, device_id=peer(j, i), device_id_type=MESH)
        return 0

    lax.fori_loop(1, strips, greet, 0)

    cell_load.wait()
    cells = cells_ref[...]
    places[...] = lax.div(lax.div(cells, LANES), packed) * LANES + lax.rem(cells, LANES)
    place_copy = pltpu.make_async_copy(places, places_ref, place_sem)
    place_copy.start()
    place_copy.wait()
    load.wait()

    def pick(j, i, put):
        target = peer(j, i)
        first = (target["rcpt"] * strips + target["space"]) * own
        for k in range(own):
            b = first + k
            for c in range(block_cells):
                picked[pl.ds(c, 1), :] = by_cell[pl.ds(places_ref[b, c], 1), :]
            turned = picked[...].T
            cell = jnp.broadcast_to(cells_ref[pl.ds(b, 1), :], (recv, block_cells))
            which = lax.rem(lax.div(cell, LANES), packed)
            for level in range(levels):
                value = turned[level * recv : (level + 1) * recv]
                for q in range(1, packed):
                    at = (q * levels + level) * recv
                    value = jnp.where(which == q, turned[at : at + recv], value)
                put(k, slice(level * block_cells, (level + 1) * block_cells), value)

    def copy_to(j, i):
        return pltpu.make_async_remote_copy(
            src_ref=sending.at[j, i], dst_ref=landed.at[strip, batch],
            send_sem=send_sem.at[j, i], recv_sem=recv_sem.at[j, i],
            device_id=peer(j, i), device_id_type=MESH,
        )

    def sample(j, i):
        def put(k, at, value):
            sending[j, i, k, :, at] = value

        pick(j, i, put)
        copy_to(j, i).start()

    pl.semaphore_wait(barrier, batches * strips - 1)

    def sample_strip(j, _):
        def one(i, _):
            sample(j, i)
            return 0

        lax.fori_loop(0, batches, one, 0)
        return 0

    lax.fori_loop(1, strips, sample_strip, 0)

    def sample_own_strip(i, _):
        sample(0, i)
        return 0

    lax.fori_loop(1, batches, sample_own_strip, 0)

    def put_own(k, at, value):
        landed[strip, batch, k, :, at] = value

    pick(0, 0, put_own)
    profile_load.wait()

    def contract(s):
        for k in range(own):
            left = landed[s, :, k].reshape(batches * recv, levels * block_cells)
            out_ref[s, k] = jnp.dot(
                left, profiles_ref[s, k], precision=lax.Precision.HIGHEST,
                preferred_element_type=jnp.float32,
            )

    def receive(j, _):
        for i in range(batches):
            copy_to(j, i).wait_recv()
        contract(lax.rem(strip + strips - j, strips))
        return 0

    lax.fori_loop(1, strips, receive, 0)
    for i in range(1, batches):
        copy_to(0, i).wait_recv()
    contract(strip)

    def sent(j, _):
        for i in range(batches):
            copy_to(j, i).wait_send()
        return 0

    lax.fori_loop(1, strips, sent, 0)
    for i in range(1, batches):
        copy_to(0, i).wait_send()


def run_response(batches, strips, recv, levels, cells, by_cell, profiles):
    blocks, block_cells = cells.shape
    own = blocks // (batches * strips)
    depth, scenarios = profiles.shape[-2:]
    vmem = pl.BlockSpec(memory_space=pltpu.VMEM)
    dma = pltpu.SemaphoreType.DMA
    return pl.pallas_call(
        functools.partial(response_kernel, batches, strips, recv, levels),
        out_shape=jax.ShapeDtypeStruct((strips, own, batches * recv, scenarios), jnp.float32),
        in_specs=[pl.BlockSpec(memory_space=pl.ANY)] * 3,
        out_specs=vmem,
        scratch_shapes=[
            pltpu.VMEM(by_cell.shape, jnp.float32),
            pltpu.VMEM(profiles.shape, jnp.float32),
            pltpu.VMEM(cells.shape, jnp.int32),
            pltpu.VMEM(cells.shape, jnp.int32),
            pltpu.SMEM(cells.shape, jnp.int32),
            pltpu.VMEM((block_cells, LANES), jnp.float32),
            pltpu.VMEM((strips, batches, own, recv, depth), jnp.float32),
            pltpu.VMEM((strips, batches, own, recv, depth), jnp.float32),
            dma,
            dma,
            dma((2,)),
            dma((strips, batches)),
            dma((strips, batches)),
        ],
        compiler_params=pltpu.CompilerParams(
            collective_id=1, has_side_effects=True, vmem_limit_bytes=VMEM_LIMIT
        ),
        name="release_response",
    )(cells, by_cell, profiles)


def on_device(
    adjoint_end, currents, plan, water_mask, mixing, decay, obs_weight, release_cells, profiles
):
    batches = lax.axis_size("rcpt")
    strips = lax.axis_size("space")
    stepped = run_steps(
        batches, strips, plan, decay, obs_weight, water_mask, mixing, adjoint_end, currents
    )
    field, by_cell = run_turn(stepped)
    recv, levels = adjoint_end.shape[:2]
    response = run_response(
        batches, strips, recv, levels, release_cells[0], by_cell, profiles
    )
    return (field, response)


def solution(mesh):
    placed = (
        P("rcpt", None, "space", None),
        P("rcpt", None, None, "space", None),
        P(),
        P("space", None),
        P(None, "space", None),
        P("rcpt"),
        P(None, "rcpt"),
        P("space", None, None),
        P(None, ("rcpt", "space"), None, None),
    )
    return jax.shard_map(
        on_device,
        mesh=mesh,
        in_specs=placed,
        out_specs=(P("rcpt", None, "space", None), P(None, ("rcpt", "space"), None, None)),
        check_vma=False,
    )
```
